32 devices in a mesh: blk: 4 (over z), src: 2 (over x), layer: 4 (over y, core).
Axes of the slice: x: 2, y: 2, z: 4, core: 2. Of those that a mesh axis runs over, the one named last changes fastest.
Arguments:
- resident_act: bfloat16 [4, 2048, 4096], P('layer', 'blk'), may hold values from -6 to 6
- resident_grad: bfloat16 [4, 2048, 4096], P('layer', 'blk'), may hold values from -6 to 6
- source_act: bfloat16 [4, 128, 4096], P('layer', ('blk', 'src')), may hold values from -6 to 6
- source_grad: bfloat16 [4, 128, 4096], P('layer', ('blk', 'src')), may hold values from -6 to 6
- probes: bfloat16 [128, 256], P(('blk', 'src')), may hold values from -6 to 6
Outputs:
- kernel_product: float32 [2048, 256], P(('blk', 'layer'))
The draws below stay inside these ranges and needn't reach their ends.
All inputs are finite; a program needn't handle non-finite values.
Results may differ from the reference program's by a relative error of at most 0.0029.
Values may be sent and summed in bfloat16 or wider, within the bound.
A program may use at most 64 MiB of HBM per device.

```python
import jax
import jax.numpy as jnp
from jax import lax

D = 4096
PROBE = 256
LAYERS = 4
RES = 2048
SOURCE = 128


def shard_levels(rng, shape, cuts, smallest, high):
    def one(position, shards_of):
        steps = jax.random.uniform(jax.random.fold_in(jax.random.fold_in(rng, 6), position), (shards_of,), jnp.float32, smallest / len(cuts), high / len(cuts))
        return jnp.repeat(jnp.exp(steps), shape[position] // shards_of).reshape((-1,) + (1,) * (len(shape) - position - 1))

    level = one(*cuts[0])
    for cut in cuts[1:]:
        level = level * one(*cut)
    return level


def bell_draw(key, shape, spread, reach, shards=(), held_as=jnp.bfloat16):
    drawn = spread * jax.random.normal(key, shape, jnp.float32)
    if shards:
        drawn = drawn * shard_levels(key, shape, shards, -0.22, 0.18)
    return jnp.clip(drawn, -reach, reach).astype(held_as)


def setup_inputs(seed: int = 0) -> dict:
    seeds = jax.random.split(jax.random.key(seed), 6)
    resident_act = bell_draw(seeds[0], (LAYERS, RES, D), 1.0, 6.0, ((0, 4), (1, 4)))
    resident_grad = bell_draw(seeds[1], (LAYERS, RES, D), 1.0, 6.0, ((0, 4), (1, 4)))
    source_act = bell_draw(seeds[2], (LAYERS, SOURCE, D), 1.0, 6.0, ((0, 4), (1, 8)))
    source_grad = bell_draw(seeds[3], (LAYERS, SOURCE, D), 1.0, 6.0, ((0, 4), (1, 8)))
    probes = bell_draw(seeds[4], (SOURCE, PROBE), 1.0, 6.0, ((0, 8),))
    return {"resident_act": resident_act, "resident_grad": resident_grad, "source_act": source_act, "source_grad": source_grad, "probes": probes}


def reference(resident_act, resident_grad, source_act, source_grad, probes):
    def one_layer(total, items):
        res_a, res_g, src_a, src_g = items
        act_gram = jnp.dot(src_a, res_a.T, preferred_element_type=jnp.float32)
        grad_gram = jnp.dot(src_g, res_g.T, preferred_element_type=jnp.float32)
        kernel = (act_gram * grad_gram * jnp.float32(1.0 / D)).astype(jnp.bfloat16)
        total = total + jnp.dot(kernel.T, probes, preferred_element_type=jnp.float32)
        return total, None

    start = jnp.zeros((RES, PROBE), jnp.float32)
    total, _ = lax.scan(one_layer, start, (resident_act, resident_grad, source_act, source_grad))
    return total * jnp.float32((LAYERS * SOURCE) ** -0.5)
```

```python
import functools

import jax
import jax.numpy as jnp
from jax import lax
from jax.experimental import pallas as pl
from jax.experimental.pallas import tpu as pltpu
from jax.sharding import PartitionSpec as P

MESH = pl.DeviceIdType.MESH


def kernel_body(
    n, groups, layers, chunks, inverse_width, scale,
    res_a, res_g, src_a, src_g, probes, out,
    res_v, src_v, probe_v, kern_v, kall,
    res_sem, own_sem, recv_sem, up_sem, down_sem,
    probe_sem, line_sem, relay_sem, kern_sem, kern_send,
):
    b = lax.axis_index("blk")
    s = lax.axis_index("src")
    l = lax.axis_index("layer")
    plane = groups * layers
    me = s * layers + l
    up = lax.rem(b + 1, n)
    down = lax.rem(b + n - 1, n)
    width = res_v.shape[2]
    step = width // chunks
    residents = (res_a, res_g)
    sources = (src_a, src_g)

    def peer(d):
        other = lax.rem(me + d, plane)
        return other, (b, other // layers, lax.rem(other, layers))

    def cols(c):
        return pl.ds(c * step, step)

    def resident_copy(a, c):
        return pltpu.make_async_copy(
            residents[a].at[0, :, cols(c)], res_v.at[a, :, cols(c)], res_sem.at[a, c]
        )

    def own_copy(a):
        return pltpu.make_async_copy(sources[a].at[0], src_v.at[a, b], own_sem.at[a])

    def move(source, a, c, block, going_up):
        return pltpu.make_async_remote_copy(
            src_ref=source,
            dst_ref=src_v.at[a, block, :, cols(c)],
            send_sem=(up_sem if going_up else down_sem).at[a, c, block],
            recv_sem=recv_sem.at[a, c, block],
            device_id=(up if going_up else down, s, l),
            device_id_type=MESH,
        )

    def forward(a, c, block, going_up):
        return move(src_v.at[a, block, :, cols(c)], a, c, block, going_up)

    def line_probe(e):
        return pltpu.make_async_remote_copy(
            src_ref=probes,
            dst_ref=probe_v.at[s, b],
            send_sem=line_sem.at[e],
            recv_sem=probe_sem.at[s, b],
            device_id=(lax.rem(b + e, n), s, l),
            device_id_type=MESH,
        )

    def own_probe():
        return pltpu.make_async_copy(probes, probe_v.at[s, b], probe_sem.at[s, b])

    def relay_probe(group, block, d):
        _, device = peer(d)
        return pltpu.make_async_remote_copy(
            src_ref=probe_v.at[group, block],
            dst_ref=probe_v.at[group, block],
            send_sem=relay_sem.at[block, d],
            recv_sem=probe_sem.at[group, block],
            device_id=device,
            device_id_type=MESH,
        )

    def kernel_slice(d):
        _, device = peer(d)
        return pltpu.make_async_remote_copy(
            src_ref=kern_v.at[device[2]],
            dst_ref=kall.at[l, s],
            send_sem=kern_send.at[d],
            recv_sem=kern_sem.at[me],
            device_id=device,
            device_id_type=MESH,
        )

    def kernel_arrival(d):
        other = lax.rem(me + d, plane)
        from_group, from_layer = other // layers, lax.rem(other, layers)
        return pltpu.make_async_remote_copy(
            src_ref=kern_v.at[0],
            dst_ref=kall.at[from_layer, from_group],
            send_sem=kern_send.at[d],
            recv_sem=kern_sem.at[other],
            device_id=(b, from_group, from_layer),
            device_id_type=MESH,
        )

    barrier = pltpu.get_barrier_semaphore()
    for d in range(1, plane):
        pl.semaphore_signal(barrier, inc=1, device_id=peer(d)[1], device_id_type=MESH)

    def greet(e, _):
        pl.semaphore_signal(
            barrier, inc=1, device_id=(lax.rem(b + e, n), s, l), device_id_type=MESH
        )
        return 0

    lax.fori_loop(1, n, greet, 0)
    for a in range(2):
        own_copy(a).start()
    for a in range(2):
        for c in range(chunks):
            resident_copy(a, c).start()
    pl.semaphore_wait(barrier, plane - 1 + n - 1)

    carries = lax.rem(b, layers) == l

    @pl.when(carries)
    def _():
        own_probe().start()

        def send(e, _):
            line_probe(e).start()
            return 0

        lax.fori_loop(1, n, send, 0)

    for a in range(2):
        for c in range(chunks):

            @pl.when(b < n - 1)
            def _():
                move(sources[a].at[0, :, cols(c)], a, c, b, True).start()

            @pl.when(b > 0)
            def _():
                move(sources[a].at[0, :, cols(c)], a, c, b, False).start()

    def forwarding(turn, _):
        low = b - 1 - turn
        high = b + 1 + turn
        for a in range(2):
            for c in range(chunks):

                @pl.when(low >= 0)
                def _():
                    forward(a, c, low, True).wait_recv()

                @pl.when(jnp.logical_and(low >= 0, b < n - 1))
                def _():
                    forward(a, c, low, True).start()

                @pl.when(high < n)
                def _():
                    forward(a, c, high, False).wait_recv()

                @pl.when(jnp.logical_and(high < n, b > 0))
                def _():
                    forward(a, c, high, False).start()

        return 0

    lax.fori_loop(0, n - 2, forwarding, 0)

    def relay(block, _):
        @pl.when(lax.rem(block, layers) == l)
        def _():
            relay_probe(s, block, 1).wait_recv()
            for d in range(1, plane):
                relay_probe(s, block, d).start()

        return 0

    lax.fori_loop(0, n, relay, 0)
    for a in range(2):
        own_copy(a).wait()

    grams = []
    for a in range(2):
        gram = None
        for c in range(chunks):

            @pl.when(b == 0)
            def _():
                forward(a, c, n - 1, False).wait_recv()

            @pl.when(b == n - 1)
            def _():
                forward(a, c, 0, True).wait_recv()

            resident_copy(a, c).wait()
            block = src_v[a, :, :, c * step:(c + 1) * step]
            part = lax.dot_general(
                block.reshape(block.shape[0] * block.shape[1], step),
                res_v[a, :, c * step:(c + 1) * step],
                (((1,), (1,)), ((), ())),
                preferred_element_type=jnp.float32,
            )
            gram = part if gram is None else gram + part
        grams.append(gram)
    kernel = (grams[0] * grams[1] * jnp.float32(inverse_width)).astype(jnp.bfloat16)
    share = kernel.shape[1] // layers
    for q in range(layers):
        kern_v[q] = kernel[:, q * share:(q + 1) * share]
    for d in range(1, plane):
        kernel_slice(d).start()
    kall[l, s] = kern_v[l]

    def arrived(i, _):
        group, block = i // n, lax.rem(i, n)

        @pl.when(jnp.logical_or(group != s, lax.rem(block, layers) != l))
        def _():
            relay_probe(group, block, 1).wait_recv()

        return 0

    lax.fori_loop(0, groups * n, arrived, 0)
    for d in range(1, plane):
        kernel_arrival(d).wait_recv()
    vectors = probe_v[...].reshape(groups * n * probe_v.shape[2], probe_v.shape[3])
    total = None
    for q in range(layers):
        part = lax.dot_general(
            kall[q].reshape(vectors.shape[0], share),
            vectors,
            (((0,), (0,)), ((), ())),
            preferred_element_type=jnp.float32,
        )
        total = part if total is None else total + part
    out[...] = total * jnp.float32(scale)

    for d in range(1, plane):
        kernel_slice(d).wait_send()

    def sent(block, _):
        @pl.when(jnp.logical_and(block <= b, b < n - 1))
        def _():
            for a in range(2):
                for c in range(chunks):
                    forward(a, c, block, True).wait_send()

        @pl.when(jnp.logical_and(block >= b, b > 0))
        def _():
            for a in range(2):
                for c in range(chunks):
                    forward(a, c, block, False).wait_send()

        @pl.when(lax.rem(block, layers) == l)
        def _():
            for d in range(1, plane):
                relay_probe(s, block, d).wait_send()

        @pl.when(jnp.logical_and(carries, block > 0))
        def _():
            line_probe(block).wait_send()

        return 0

    lax.fori_loop(0, n, sent, 0)


def on_device(resident_act, resident_grad, source_act, source_grad, probes):
    n = lax.axis_size("blk")
    groups = lax.axis_size("src")
    layers = lax.axis_size("layer")
    _, rows, width = resident_act.shape
    per = source_act.shape[1]
    columns = probes.shape[1]
    source_total = per * n * groups
    total_layers = resident_act.shape[0] * layers
    share = rows // layers
    plane = groups * layers
    chunks = max(1, min(4, 16 // n))
    body = functools.partial(
        kernel_body, n, groups, layers, chunks, 1.0 / width,
        (total_layers * source_total) ** (-0.5),
    )
    dma = pltpu.SemaphoreType.DMA
    return pl.pallas_call(
        body,
        out_shape=jax.ShapeDtypeStruct((share, columns), jnp.float32),
        in_specs=[pl.BlockSpec(memory_space=pl.ANY)] * 5,
        out_specs=pl.BlockSpec(memory_space=pltpu.VMEM),
        scratch_shapes=[
            pltpu.VMEM((2, rows, width), jnp.bfloat16),
            pltpu.VMEM((2, n, per, width), jnp.bfloat16),
            pltpu.VMEM((groups, n, per, columns), jnp.bfloat16),
            pltpu.VMEM((layers, n * per, share), jnp.bfloat16),
            pltpu.VMEM((layers, groups, n * per, share), jnp.bfloat16),
            dma((2, chunks)),
            dma((2,)),
            dma((2, chunks, n)),
            dma((2, chunks, n)),
            dma((2, chunks, n)),
            dma((groups, n)),
            dma((n,)),
            dma((n, plane)),
            dma((plane,)),
            dma((plane,)),
        ],
        compiler_params=pltpu.CompilerParams(
            collective_id=0, has_side_effects=True, vmem_limit_bytes=56 * 1024 * 1024
        ),
        cost_estimate=pl.CostEstimate(
            flops=4 * n * per * rows * width,
            bytes_accessed=4 * rows * width,
            transcendentals=0,
        ),
        name="ntk_product",
    )(resident_act, resident_grad, source_act, source_grad, probes)


def solution(mesh):
    in_specs = (
        P("layer", "blk", None),
        P("layer", "blk", None),
        P("layer", ("blk", "src"), None),
        P("layer", ("blk", "src"), None),
        P(("blk", "src"), None),
    )
    out_specs = P(("blk", "layer"), None)
    return jax.shard_map(
        on_device, mesh=mesh, in_specs=in_specs, out_specs=out_specs, check_vma=False
    )
```

```python
import functools

import jax
import jax.numpy as jnp
from jax import lax
from jax.experimental import pallas as pl
from jax.experimental.pallas import tpu as pltpu
from jax.sharding import PartitionSpec as P

MESH = pl.DeviceIdType.MESH


def kernel_body(
    n, groups, layers, chunks, flight, inverse_width, scale,
    res_a, res_g, src_a, src_g, probes, out,
    res_v, src_v, probe_v, near_v, far_v, near_all, far_all,
    res_sem, own_sem, recv_sem, up_sem, down_sem,
    probe_sem, line_up, line_down, relay_sem,
    near_sem, near_send, far_sem, far_send,
):
    b = lax.axis_index("blk")
    s = lax.axis_index("src")
    l = lax.axis_index("layer")
    plane = groups * layers
    me = s * layers + l
    up = lax.rem(b + 1, n)
    down = lax.rem(b + n - 1, n)
    width = res_v.shape[2]
    step = width // chunks
    residents = (res_a, res_g)
    sources = (src_a, src_g)
    items = [(a, c) for a in range(2) for c in range(chunks)]
    has_up = b < n - 1
    has_down = b > 0

    def slot(position, block):
        return jnp.where(2 * position < n, block, n - 1 - block)

    def device_of(other):
        return (b, other // layers, lax.rem(other, layers))

    def peer(d):
        return device_of(lax.rem(me + d, plane))

    def cols(c):
        return pl.ds(c * step, step)

    def resident_copy(a, c):
        return pltpu.make_async_copy(
            residents[a].at[0, :, cols(c)], res_v.at[a, :, cols(c)], res_sem.at[a, c]
        )

    def own_copy(a):
        return pltpu.make_async_copy(
            sources[a].at[0], src_v.at[a, slot(b, b)], own_sem.at[a]
        )

    def move(source, a, c, block, going_up):
        to = up if going_up else down
        return pltpu.make_async_remote_copy(
            src_ref=source,
            dst_ref=src_v.at[a, slot(to, block), :, cols(c)],
            send_sem=(up_sem if going_up else down_sem).at[a, c, block],
            recv_sem=recv_sem.at[a, c, block],
            device_id=(to, s, l),
            device_id_type=MESH,
        )

    def own(a, c, going_up):
        return move(sources[a].at[0, :, cols(c)], a, c, b, going_up)

    def forward(a, c, block, going_up):
        return move(src_v.at[a, slot(b, block), :, cols(c)], a, c, block, going_up)

    def arrive(a, c, block):
        here = src_v.at[a, slot(b, block), :, cols(c)]
        return pltpu.make_async_copy(here, here, recv_sem.at[a, c, block])

    def line_probe(block, going_up, source=None):
        to = up if going_up else down
        return pltpu.make_async_remote_copy(
            src_ref=probe_v.at[s, slot(b, block)] if source is None else source,
            dst_ref=probe_v.at[s, slot(to, block)],
            send_sem=(line_up if going_up else line_down).at[block],
            recv_sem=probe_sem.at[s, block],
            device_id=(to, s, l),
            device_id_type=MESH,
        )

    def own_probe():
        return pltpu.make_async_copy(
            probes, probe_v.at[s, slot(b, b)], probe_sem.at[s, b]
        )

    def probe_arrive(group, block):
        here = probe_v.at[group, slot(b, block)]
        return pltpu.make_async_copy(here, here, probe_sem.at[group, block])

    def relay_probe(block, d):
        here = probe_v.at[s, slot(b, block)]
        return pltpu.make_async_remote_copy(
            src_ref=here,
            dst_ref=here,
            send_sem=relay_sem.at[block, d],
            recv_sem=probe_sem.at[s, block],
            device_id=peer(d),
            device_id_type=MESH,
        )

    def kernel_slice(d, far):
        device = peer(d)
        return pltpu.make_async_remote_copy(
            src_ref=(far_v if far else near_v).at[device[2]],
            dst_ref=(far_all if far else near_all).at[l, s],
            send_sem=(far_send if far else near_send).at[d],
            recv_sem=(far_sem if far else near_sem).at[me],
            device_id=device,
            device_id_type=MESH,
        )

    def kernel_arrive(d, far):
        other = lax.rem(me + d, plane)
        _, from_group, from_layer = device_of(other)
        here = (far_all if far else near_all).at[from_layer, from_group]
        return pltpu.make_async_copy(here, here, (far_sem if far else near_sem).at[other])

    def signal(device):
        pl.semaphore_signal(
            pltpu.get_barrier_semaphore(), inc=1, device_id=device, device_id_type=MESH
        )

    @pl.when(has_down)
    def _():
        signal((down, s, l))

    @pl.when(has_up)
    def _():
        signal((up, s, l))

    for d in range(1, plane):
        signal(peer(d))
    carries = lax.rem(b, layers) == l

    @pl.when(carries)
    def _():
        own_probe().start()

    for a in range(2):
        own_copy(a).start()
    for a, c in items:
        resident_copy(a, c).start()
    pl.semaphore_wait(
        pltpu.get_barrier_semaphore(),
        plane - 1 + has_up.astype(jnp.int32) + has_down.astype(jnp.int32),
    )

    @pl.when(jnp.logical_and(carries, has_down))
    def _():
        line_probe(b, False, probes).start()

    @pl.when(jnp.logical_and(carries, has_up))
    def _():
        line_probe(b, True, probes).start()

    for k, (a, c) in enumerate(items):
        for going_up, has in ((False, has_down), (True, has_up)):

            @pl.when(has)
            def _():
                if k >= flight:
                    forward(*items[k - flight], b, going_up).wait_send()
                own(a, c, going_up).start()

    def forwarding(turn, _):
        low = b - 1 - turn
        high = b + 1 + turn
        for block, inside, going_up, has in (
            (high, high < n, False, has_down),
            (low, low >= 0, True, has_up),
        ):
            probe_here = jnp.logical_and(inside, lax.rem(jnp.maximum(block, 0), layers) == l)

            @pl.when(probe_here)
            def _():
                probe_arrive(s, block).wait()

            @pl.when(jnp.logical_and(probe_here, has))
            def _():
                line_probe(block, going_up).start()

        for k, (a, c) in enumerate(items):
            for block, inside, going_up, has in (
                (high, high < n, False, has_down),
                (low, low >= 0, True, has_up),
            ):
                before = items[k - flight]
                earlier = block if k >= flight else (block + 1 if going_up else block - 1)

                @pl.when(inside)
                def _():
                    arrive(a, c, block).wait()

                @pl.when(jnp.logical_and(inside, has))
                def _():
                    forward(*before, earlier, going_up).wait_send()
                    forward(a, c, block, going_up).start()

        return 0

    lax.fori_loop(0, n - 2, forwarding, 0)
    for a in range(2):
        own_copy(a).wait()

    def product(grams, buffer):
        kernel = (grams[0] * grams[1] * jnp.float32(inverse_width)).astype(jnp.bfloat16)
        share = kernel.shape[1] // layers
        for q in range(layers):
            buffer[q] = kernel[:, q * share:(q + 1) * share]

    def gram(a, far):
        total = None
        for c in range(chunks):
            if far:

                @pl.when(b == 0)
                def _():
                    arrive(a, c, n - 1).wait()

                @pl.when(b == n - 1)
                def _():
                    arrive(a, c, 0).wait()

                block = src_v[a, n - 1, :, c * step:(c + 1) * step]
            else:
                resident_copy(a, c).wait()
                block = src_v[a, 0:n - 1, :, c * step:(c + 1) * step]
                block = block.reshape(block.shape[0] * block.shape[1], step)
            part = lax.dot_general(
                block,
                res_v[a, :, c * step:(c + 1) * step],
                (((1,), (1,)), ((), ())),
                preferred_element_type=jnp.float32,
            )
            total = part if total is None else total + part
        return total

    product([gram(a, False) for a in range(2)], near_v)
    for d in range(1, plane):
        kernel_slice(d, False).start()
    near_all[l, s] = near_v[l]

    def relay(block, _):
        @pl.when(lax.rem(block, layers) == l)
        def _():
            at_end = jnp.logical_or(
                jnp.logical_and(b == 0, block == n - 1),
                jnp.logical_and(b == n - 1, block == 0),
            )

            @pl.when(jnp.logical_or(block == b, at_end))
            def _():
                probe_arrive(s, block).wait()

            for d in range(1, plane):
                relay_probe(block, d).start()

        return 0

    lax.fori_loop(0, n, relay, 0)

    product([gram(a, True) for a in range(2)], far_v)
    for d in range(1, plane):
        kernel_slice(d, True).start()
    far_all[l, s] = far_v[l]

    def arrived(i, _):
        group, block = i // n, lax.rem(i, n)

        @pl.when(jnp.logical_or(group != s, lax.rem(block, layers) != l))
        def _():
            probe_arrive(group, block).wait()

        return 0

    lax.fori_loop(0, groups * n, arrived, 0)

    def contract(everything, vectors):
        depth, columns = vectors.shape[0] * vectors.shape[1], vectors.shape[2]
        total = None
        for q in range(layers):
            part = lax.dot_general(
                everything[q].reshape(depth, everything.shape[3]),
                vectors.reshape(depth, columns),
                (((0,), (0,)), ((), ())),
                preferred_element_type=jnp.float32,
            )
            total = part if total is None else total + part
        return total

    for d in range(1, plane):
        kernel_arrive(d, False).wait()
    near_vectors = probe_v[:, 0:n - 1]
    near = contract(
        near_all,
        near_vectors.reshape(groups, (n - 1) * probe_v.shape[2], probe_v.shape[3]),
    )

    def sent(block, _):
        @pl.when(lax.rem(block, layers) == l)
        def _():
            for d in range(1, plane):
                relay_probe(block, d).wait_send()

            @pl.when(jnp.logical_and(has_up, block <= b))
            def _():
                line_probe(block, True).wait_send()

            @pl.when(jnp.logical_and(has_down, block >= b))
            def _():
                line_probe(block, False).wait_send()

        return 0

    lax.fori_loop(0, n, sent, 0)
    for block, going_up, has in ((n - 1, False, has_down), (0, True, has_up)):

        @pl.when(has)
        def _():
            for a, c in items[-flight:]:
                forward(a, c, block, going_up).wait_send()

    for d in range(1, plane):
        kernel_slice(d, False).wait_send()
    for d in range(1, plane):
        kernel_arrive(d, True).wait()
    out[...] = (near + contract(far_all, probe_v[:, n - 1])) * jnp.float32(scale)
    for d in range(1, plane):
        kernel_slice(d, True).wait_send()


def on_device(resident_act, resident_grad, source_act, source_grad, probes):
    n = lax.axis_size("blk")
    groups = lax.axis_size("src")
    layers = lax.axis_size("layer")
    _, rows, width = resident_act.shape
    per = source_act.shape[1]
    columns = probes.shape[1]
    source_total = per * n * groups
    total_layers = resident_act.shape[0] * layers
    share = rows // layers
    plane = groups * layers
    chunks = max(1, min(4, 16 // n))
    flight = min(3, 2 * chunks)
    body = functools.partial(
        kernel_body, n, groups, layers, chunks, flight, 1.0 / width,
        (total_layers * source_total) ** (-0.5),
    )
    dma = pltpu.SemaphoreType.DMA
    return pl.pallas_call(
        body,
        out_shape=jax.ShapeDtypeStruct((share, columns), jnp.float32),
        in_specs=[pl.BlockSpec(memory_space=pl.ANY)] * 5,
        out_specs=pl.BlockSpec(memory_space=pltpu.VMEM),
        scratch_shapes=[
            pltpu.VMEM((2, rows, width), jnp.bfloat16),
            pltpu.VMEM((2, n, per, width), jnp.bfloat16),
            pltpu.VMEM((groups, n, per, columns), jnp.bfloat16),
            pltpu.VMEM((layers, (n - 1) * per, share), jnp.bfloat16),
            pltpu.VMEM((layers, per, share), jnp.bfloat16),
            pltpu.VMEM((layers, groups, (n - 1) * per, share), jnp.bfloat16),
            pltpu.VMEM((layers, groups, per, share), jnp.bfloat16),
            dma((2, chunks)),
            dma((2,)),
            dma((2, chunks, n)),
            dma((2, chunks, n)),
            dma((2, chunks, n)),
            dma((groups, n)),
            dma((n,)),
            dma((n,)),
            dma((n, plane)),
            dma((plane,)),
            dma((plane,)),
            dma((plane,)),
            dma((plane,)),
        ],
        compiler_params=pltpu.CompilerParams(
            collective_id=0, has_side_effects=True, vmem_limit_bytes=56 * 1024 * 1024
        ),
        cost_estimate=pl.CostEstimate(
            flops=4 * n * per * rows * width,
            bytes_accessed=4 * rows * width,
            transcendentals=0,
        ),
        name="ntk_product",
    )(resident_act, resident_grad, source_act, source_grad, probes)


def solution(mesh):
    in_specs = (
        P("layer", "blk", None),
        P("layer", "blk", None),
        P("layer", ("blk", "src"), None),
        P("layer", ("blk", "src"), None),
        P(("blk", "src"), None),
    )
    out_specs = P(("blk", "layer"), None)
    return jax.shard_map(
        on_device, mesh=mesh, in_specs=in_specs, out_specs=out_specs, check_vma=False
    )
```

```python
import functools

import jax
import jax.numpy as jnp
from jax import lax
from jax.experimental import pallas as pl
from jax.experimental.pallas import tpu as pltpu
from jax.sharding import PartitionSpec as P

MESH = pl.DeviceIdType.MESH


def kernel_body(
    n, groups, layers, chunks, flight, inverse_width, scale,
    res_a, res_g, src_a, src_g, probes, out,
    res_v, src_v, probe_v, near_v, far_v, near_all, far_all,
    res_sem, own_sem, recv_sem, up_sem, down_sem,
    probe_sem, line_up, line_down, relay_sem,
    near_sem, near_send, far_sem, far_send,
):
    b = lax.axis_index("blk")
    s = lax.axis_index("src")
    l = lax.axis_index("layer")
    plane = groups * layers
    me = s * layers + l
    up = lax.rem(b + 1, n)
    down = lax.rem(b + n - 1, n)
    width = res_v.shape[2]
    step = width // chunks
    residents = (res_a, res_g)
    sources = (src_a, src_g)
    items = [(a, c) for a in range(2) for c in range(chunks)]
    has_up = b < n - 1
    has_down = b > 0

    def slot(position, block):
        return jnp.where(2 * position < n, block, n - 1 - block)

    def device_of(other):
        return (b, other // layers, lax.rem(other, layers))

    def peer(d):
        return device_of(lax.rem(me + d, plane))

    def cols(c):
        return pl.ds(c * step, step)

    def resident_copy(a, c):
        return pltpu.make_async_copy(
            residents[a].at[0, :, cols(c)], res_v.at[a, :, cols(c)], res_sem.at[a, c]
        )

    def own_copy(a):
        return pltpu.make_async_copy(
            sources[a].at[0], src_v.at[a, slot(b, b)], own_sem.at[a]
        )

    def move(source, a, c, block, going_up):
        to = up if going_up else down
        return pltpu.make_async_remote_copy(
            src_ref=source,
            dst_ref=src_v.at[a, slot(to, block), :, cols(c)],
            send_sem=(up_sem if going_up else down_sem).at[a, c, block],
            recv_sem=recv_sem.at[a, c, block],
            device_id=(to, s, l),
            device_id_type=MESH,
        )

    def own(a, c, going_up):
        return move(sources[a].at[0, :, cols(c)], a, c, b, going_up)

    def forward(a, c, block, going_up):
        return move(src_v.at[a, slot(b, block), :, cols(c)], a, c, block, going_up)

    def arrive(a, c, block):
        here = src_v.at[a, slot(b, block), :, cols(c)]
        return pltpu.make_async_copy(here, here, recv_sem.at[a, c, block])

    def line_probe(block, going_up, source=None):
        to = up if going_up else down
        return pltpu.make_async_remote_copy(
            src_ref=probe_v.at[s, slot(b, block)] if source is None else source,
            dst_ref=probe_v.at[s, slot(to, block)],
            send_sem=(line_up if going_up else line_down).at[block],
            recv_sem=probe_sem.at[s, block],
            device_id=(to, s, l),
            device_id_type=MESH,
        )

    def own_probe():
        return pltpu.make_async_copy(
            probes, probe_v.at[s, slot(b, b)], probe_sem.at[s, b]
        )

    def probe_arrive(group, block):
        here = probe_v.at[group, slot(b, block)]
        return pltpu.make_async_copy(here, here, probe_sem.at[group, block])

    def relay_probe(block, d):
        here = probe_v.at[s, slot(b, block)]
        return pltpu.make_async_remote_copy(
            src_ref=here,
            dst_ref=here,
            send_sem=relay_sem.at[block, d],
            recv_sem=probe_sem.at[s, block],
            device_id=peer(d),
            device_id_type=MESH,
        )

    def kernel_slice(d, far):
        device = peer(d)
        return pltpu.make_async_remote_copy(
            src_ref=(far_v if far else near_v).at[device[2]],
            dst_ref=(far_all if far else near_all).at[l, s],
            send_sem=(far_send if far else near_send).at[d],
            recv_sem=(far_sem if far else near_sem).at[me],
            device_id=device,
            device_id_type=MESH,
        )

    def kernel_arrive(d, far):
        other = lax.rem(me + d, plane)
        _, from_group, from_layer = device_of(other)
        here = (far_all if far else near_all).at[from_layer, from_group]
        return pltpu.make_async_copy(here, here, (far_sem if far else near_sem).at[other])

    def signal(device):
        pl.semaphore_signal(
            pltpu.get_barrier_semaphore(), inc=1, device_id=device, device_id_type=MESH
        )

    @pl.when(has_down)
    def _():
        signal((down, s, l))

    @pl.when(has_up)
    def _():
        signal((up, s, l))

    for d in range(1, plane):
        signal(peer(d))
    carries = lax.rem(b, layers) == l

    @pl.when(carries)
    def _():
        own_probe().start()

    for a in range(2):
        own_copy(a).start()
    for a, c in items:
        resident_copy(a, c).start()
    pl.semaphore_wait(
        pltpu.get_barrier_semaphore(),
        plane - 1 + has_up.astype(jnp.int32) + has_down.astype(jnp.int32),
    )

    @pl.when(jnp.logical_and(carries, has_down))
    def _():
        line_probe(b, False, probes).start()

    @pl.when(jnp.logical_and(carries, has_up))
    def _():
        line_probe(b, True, probes).start()

    for k, (a, c) in enumerate(items):
        for going_up, has in ((False, has_down), (True, has_up)):

            @pl.when(has)
            def _():
                if k >= flight:
                    forward(*items[k - flight], b, going_up).wait_send()
                own(a, c, going_up).start()

    def forwarding(turn, _):
        low = b - 1 - turn
        high = b + 1 + turn
        for block, inside, going_up, has in (
            (high, high < n, False, has_down),
            (low, low >= 0, True, has_up),
        ):
            probe_here = jnp.logical_and(inside, lax.rem(jnp.maximum(block, 0), layers) == l)

            @pl.when(probe_here)
            def _():
                probe_arrive(s, block).wait()

            @pl.when(jnp.logical_and(probe_here, has))
            def _():
                line_probe(block, going_up).start()

        for k, (a, c) in enumerate(items):
            for block, inside, going_up, has in (
                (high, high < n, False, has_down),
                (low, low >= 0, True, has_up),
            ):
                before = items[k - flight]
                earlier = block if k >= flight else (block + 1 if going_up else block - 1)

                @pl.when(inside)
                def _():
                    arrive(a, c, block).wait()

                @pl.when(jnp.logical_and(inside, has))
                def _():
                    forward(*before, earlier, going_up).wait_send()
                    forward(a, c, block, going_up).start()

        return 0

    lax.fori_loop(0, n - 2, forwarding, 0)
    for a in range(2):
        own_copy(a).wait()

    def product(grams, buffer):
        kernel = (grams[0] * grams[1] * jnp.float32(inverse_width)).T.astype(jnp.bfloat16)
        share = kernel.shape[1] // layers
        for q in range(layers):
            buffer[q] = kernel[:, q * share:(q + 1) * share]

    def gram(a, far):
        total = None
        for c in range(chunks):
            if far:

                @pl.when(b == 0)
                def _():
                    arrive(a, c, n - 1).wait()

                @pl.when(b == n - 1)
                def _():
                    arrive(a, c, 0).wait()

                block = src_v[a, n - 1, :, c * step:(c + 1) * step]
            else:
                resident_copy(a, c).wait()
                block = src_v[a, 0:n - 1, :, c * step:(c + 1) * step]
                block = block.reshape(block.shape[0] * block.shape[1], step)
            part = lax.dot_general(
                res_v[a, :, c * step:(c + 1) * step],
                block,
                (((1,), (1,)), ((), ())),
                preferred_element_type=jnp.float32,
            )
            total = part if total is None else total + part
        return total

    product([gram(a, False) for a in range(2)], near_v)
    for d in range(1, plane):
        kernel_slice(d, False).start()
    near_all[l, s] = near_v[l]

    def relay(block, _):
        @pl.when(lax.rem(block, layers) == l)
        def _():
            at_end = jnp.logical_or(
                jnp.logical_and(b == 0, block == n - 1),
                jnp.logical_and(b == n - 1, block == 0),
            )

            @pl.when(jnp.logical_or(block == b, at_end))
            def _():
                probe_arrive(s, block).wait()

            for d in range(1, plane):
                relay_probe(block, d).start()

        return 0

    lax.fori_loop(0, n, relay, 0)

    product([gram(a, True) for a in range(2)], far_v)
    for d in range(1, plane):
        kernel_slice(d, True).start()
    far_all[l, s] = far_v[l]

    def arrived(i, _):
        group, block = i // n, lax.rem(i, n)

        @pl.when(jnp.logical_or(group != s, lax.rem(block, layers) != l))
        def _():
            probe_arrive(group, block).wait()

        return 0

    lax.fori_loop(0, groups * n, arrived, 0)

    def contract(everything, vectors):
        depth, columns = vectors.shape[0] * vectors.shape[1], vectors.shape[2]
        total = None
        for q in range(layers):
            part = lax.dot_general(
                everything[q].reshape(depth, everything.shape[3]),
                vectors.reshape(depth, columns),
                (((0,), (0,)), ((), ())),
                preferred_element_type=jnp.float32,
            )
            total = part if total is None else total + part
        return total

    for d in range(1, plane):
        kernel_arrive(d, False).wait()
    near_vectors = probe_v[:, 0:n - 1]
    near = contract(
        near_all,
        near_vectors.reshape(groups, (n - 1) * probe_v.shape[2], probe_v.shape[3]),
    )

    def sent(block, _):
        @pl.when(lax.rem(block, layers) == l)
        def _():
            for d in range(1, plane):
                relay_probe(block, d).wait_send()

            @pl.when(jnp.logical_and(has_up, block <= b))
            def _():
                line_probe(block, True).wait_send()

            @pl.when(jnp.logical_and(has_down, block >= b))
            def _():
                line_probe(block, False).wait_send()

        return 0

    lax.fori_loop(0, n, sent, 0)
    for block, going_up, has in ((n - 1, False, has_down), (0, True, has_up)):

        @pl.when(has)
        def _():
            for a, c in items[-flight:]:
                forward(a, c, block, going_up).wait_send()

    for d in range(1, plane):
        kernel_slice(d, False).wait_send()
    for d in range(1, plane):
        kernel_arrive(d, True).wait()
    out[...] = (near + contract(far_all, probe_v[:, n - 1])) * jnp.float32(scale)
    for d in range(1, plane):
        kernel_slice(d, True).wait_send()


def on_device(resident_act, resident_grad, source_act, source_grad, probes):
    n = lax.axis_size("blk")
    groups = lax.axis_size("src")
    layers = lax.axis_size("layer")
    _, rows, width = resident_act.shape
    per = source_act.shape[1]
    columns = probes.shape[1]
    source_total = per * n * groups
    total_layers = resident_act.shape[0] * layers
    share = rows // layers
    plane = groups * layers
    chunks = max(1, min(4, 16 // n))
    flight = min(3, 2 * chunks)
    body = functools.partial(
        kernel_body, n, groups, layers, chunks, flight, 1.0 / width,
        (total_layers * source_total) ** (-0.5),
    )
    dma = pltpu.SemaphoreType.DMA
    return pl.pallas_call(
        body,
        out_shape=jax.ShapeDtypeStruct((share, columns), jnp.float32),
        in_specs=[pl.BlockSpec(memory_space=pl.ANY)] * 5,
        out_specs=pl.BlockSpec(memory_space=pltpu.VMEM),
        scratch_shapes=[
            pltpu.VMEM((2, rows, width), jnp.bfloat16),
            pltpu.VMEM((2, n, per, width), jnp.bfloat16),
            pltpu.VMEM((groups, n, per, columns), jnp.bfloat16),
            pltpu.VMEM((layers, (n - 1) * per, share), jnp.bfloat16),
            pltpu.VMEM((layers, per, share), jnp.bfloat16),
            pltpu.VMEM((layers, groups, (n - 1) * per, share), jnp.bfloat16),
            pltpu.VMEM((layers, groups, per, share), jnp.bfloat16),
            dma((2, chunks)),
            dma((2,)),
            dma((2, chunks, n)),
            dma((2, chunks, n)),
            dma((2, chunks, n)),
            dma((groups, n)),
            dma((n,)),
            dma((n,)),
            dma((n, plane)),
            dma((plane,)),
            dma((plane,)),
            dma((plane,)),
            dma((plane,)),
        ],
        compiler_params=pltpu.CompilerParams(
            collective_id=0, has_side_effects=True, vmem_limit_bytes=56 * 1024 * 1024
        ),
        cost_estimate=pl.CostEstimate(
            flops=4 * n * per * rows * width,
            bytes_accessed=4 * rows * width,
            transcendentals=0,
        ),
        name="ntk_product",
    )(resident_act, resident_grad, source_act, source_grad, probes)


def solution(mesh):
    in_specs = (
        P("layer", "blk", None),
        P("layer", "blk", None),
        P("layer", ("blk", "src"), None),
        P("layer", ("blk", "src"), None),
        P(("blk", "src"), None),
    )
    out_specs = P(("blk", "layer"), None)
    return jax.shard_map(
        on_device, mesh=mesh, in_specs=in_specs, out_specs=out_specs, check_vma=False
    )
```

```python
import functools

import jax
import jax.numpy as jnp
from jax import lax
from jax.experimental import pallas as pl
from jax.experimental.pallas import tpu as pltpu
from jax.sharding import PartitionSpec as P

MESH = pl.DeviceIdType.MESH


def kernel_body(
    n, groups, layers, chunks, flight, inverse_width, scale,
    res_a, res_g, src_a, src_g, probes, out,
    res_v, src_v, probe_v, near_v, far_v, near_all, far_all,
    res_sem, own_sem, recv_sem, up_sem, down_sem,
    probe_sem, line_up, line_down, relay_sem,
    near_sem, near_send, far_sem, far_send,
):
    b = lax.axis_index("blk")
    s = lax.axis_index("src")
    l = lax.axis_index("layer")
    plane = groups * layers
    me = s * layers + l
    up = lax.rem(b + 1, n)
    down = lax.rem(b + n - 1, n)
    width = res_v.shape[2]
    step = width // chunks
    residents = (res_a, res_g)
    sources = (src_a, src_g)
    items = [(a, c) for a in range(2) for c in range(chunks)]
    has_up = b < n - 1
    has_down = b > 0

    def slot(position, block):
        return jnp.where(2 * position < n, block, n - 1 - block)

    def device_of(other):
        return (b, other // layers, lax.rem(other, layers))

    def peer(d):
        return device_of(lax.rem(me + d, plane))

    def cols(c):
        return pl.ds(c * step, step)

    def resident_copy(a, c):
        return pltpu.make_async_copy(
            residents[a].at[0, :, cols(c)], res_v.at[a, :, cols(c)], res_sem.at[a, c]
        )

    def own_copy(a):
        return pltpu.make_async_copy(
            sources[a].at[0], src_v.at[a, slot(b, b)], own_sem.at[a]
        )

    def move(source, a, c, block, going_up):
        to = up if going_up else down
        return pltpu.make_async_remote_copy(
            src_ref=source,
            dst_ref=src_v.at[a, slot(to, block), :, cols(c)],
            send_sem=(up_sem if going_up else down_sem).at[a, c, block],
            recv_sem=recv_sem.at[a, c, block],
            device_id=(to, s, l),
            device_id_type=MESH,
        )

    def own(a, c, going_up):
        return move(sources[a].at[0, :, cols(c)], a, c, b, going_up)

    def forward(a, c, block, going_up):
        return move(src_v.at[a, slot(b, block), :, cols(c)], a, c, block, going_up)

    def arrive(a, c, block):
        here = src_v.at[a, slot(b, block), :, cols(c)]
        return pltpu.make_async_copy(here, here, recv_sem.at[a, c, block])

    def line_probe(block, going_up, source=None):
        to = up if going_up else down
        return pltpu.make_async_remote_copy(
            src_ref=probe_v.at[s, slot(b, block)] if source is None else source,
            dst_ref=probe_v.at[s, slot(to, block)],
            send_sem=(line_up if going_up else line_down).at[block],
            recv_sem=probe_sem.at[s, block],
            device_id=(to, s, l),
            device_id_type=MESH,
        )

    def own_probe():
        return pltpu.make_async_copy(
            probes, probe_v.at[s, slot(b, b)], probe_sem.at[s, b]
        )

    def probe_arrive(group, block):
        here = probe_v.at[group, slot(b, block)]
        return pltpu.make_async_copy(here, here, probe_sem.at[group, block])

    def relay_probe(block, d):
        here = probe_v.at[s, slot(b, block)]
        return pltpu.make_async_remote_copy(
            src_ref=here,
            dst_ref=here,
            send_sem=relay_sem.at[block, d],
            recv_sem=probe_sem.at[s, block],
            device_id=peer(d),
            device_id_type=MESH,
        )

    def kernel_slice(d, far):
        device = peer(d)
        return pltpu.make_async_remote_copy(
            src_ref=(far_v if far else near_v).at[device[2]],
            dst_ref=(far_all if far else near_all).at[l, s],
            send_sem=(far_send if far else near_send).at[d],
            recv_sem=(far_sem if far else near_sem).at[me],
            device_id=device,
            device_id_type=MESH,
        )

    def kernel_arrive(d, far):
        other = lax.rem(me + d, plane)
        _, from_group, from_layer = device_of(other)
        here = (far_all if far else near_all).at[from_layer, from_group]
        return pltpu.make_async_copy(here, here, (far_sem if far else near_sem).at[other])

    def signal(device):
        pl.semaphore_signal(
            pltpu.get_barrier_semaphore(), inc=1, device_id=device, device_id_type=MESH
        )

    @pl.when(has_down)
    def _():
        signal((down, s, l))

    @pl.when(has_up)
    def _():
        signal((up, s, l))

    for d in range(1, plane):
        signal(peer(d))
    carries = lax.rem(b, layers) == l

    @pl.when(carries)
    def _():
        own_probe().start()

    for a in range(2):
        own_copy(a).start()
    for a, c in items:
        resident_copy(a, c).start()
    pl.semaphore_wait(
        pltpu.get_barrier_semaphore(),
        plane - 1 + has_up.astype(jnp.int32) + has_down.astype(jnp.int32),
    )

    @pl.when(jnp.logical_and(carries, has_down))
    def _():
        line_probe(b, False, probes).start()

    @pl.when(jnp.logical_and(carries, has_up))
    def _():
        line_probe(b, True, probes).start()

    for k, (a, c) in enumerate(items):
        for going_up, has in ((False, has_down), (True, has_up)):

            @pl.when(has)
            def _():
                if k >= flight:
                    forward(*items[k - flight], b, going_up).wait_send()
                own(a, c, going_up).start()

    def forwarding(turn, _):
        low = b - 1 - turn
        high = b + 1 + turn
        for block, inside, going_up, has in (
            (high, high < n, False, has_down),
            (low, low >= 0, True, has_up),
        ):
            probe_here = jnp.logical_and(inside, lax.rem(jnp.maximum(block, 0), layers) == l)

            @pl.when(probe_here)
            def _():
                probe_arrive(s, block).wait()

            @pl.when(jnp.logical_and(probe_here, has))
            def _():
                line_probe(block, going_up).start()

        for k, (a, c) in enumerate(items):
            for block, inside, going_up, has in (
                (high, high < n, False, has_down),
                (low, low >= 0, True, has_up),
            ):
                before = items[k - flight]
                earlier = block if k >= flight else (block + 1 if going_up else block - 1)

                @pl.when(inside)
                def _():
                    arrive(a, c, block).wait()

                @pl.when(jnp.logical_and(inside, has))
                def _():
                    forward(*before, earlier, going_up).wait_send()
                    forward(a, c, block, going_up).start()

        return 0

    at_end = jnp.logical_or(b == 0, b == n - 1)
    lax.fori_loop(0, n - 3, forwarding, 0)
    for a in range(2):
        own_copy(a).wait()

    def product(grams, buffers):
        kernel = (grams[0] * grams[1] * jnp.float32(inverse_width)).astype(jnp.bfloat16)
        share = kernel.shape[1] // layers
        row = 0
        for buffer in buffers:
            rows = buffer.shape[1]
            for q in range(layers):
                buffer[q] = kernel[row:row + rows, q * share:(q + 1) * share]
            row += rows

    def gram(a, first, last, ready):
        total = None
        for c in range(chunks):
            ready(a, c)
            block = src_v[a, first:last, :, c * step:(c + 1) * step]
            part = lax.dot_general(
                block.reshape(block.shape[0] * block.shape[1], step),
                res_v[a, :, c * step:(c + 1) * step],
                (((1,), (1,)), ((), ())),
                preferred_element_type=jnp.float32,
            )
            total = part if total is None else total + part
        return total

    def resident_ready(a, c):
        resident_copy(a, c).wait()

    def farthest_ready(a, c):
        for distance in (n - 2, n - 1):
            arrive(a, c, jnp.where(b == 0, distance, n - 1 - distance)).wait()

    @pl.when(at_end)
    def _():
        product([gram(a, 0, n - 2, resident_ready) for a in range(2)], (near_v,))
        for d in range(1, plane):
            kernel_slice(d, False).start()

    @pl.when(jnp.logical_not(at_end))
    def _():
        forwarding(n - 3, 0)

    def relay(block, _):
        @pl.when(lax.rem(block, layers) == l)
        def _():
            gap = jnp.abs(block - b)
            unseen = jnp.logical_and(at_end, gap >= n - 2)

            @pl.when(jnp.logical_or(block == b, unseen))
            def _():
                probe_arrive(s, block).wait()

            for d in range(1, plane):
                relay_probe(block, d).start()

        return 0

    lax.fori_loop(0, n, relay, 0)

    @pl.when(at_end)
    def _():
        product([gram(a, n - 2, n, farthest_ready) for a in range(2)], (far_v,))

    @pl.when(jnp.logical_not(at_end))
    def _():
        product([gram(a, 0, n, resident_ready) for a in range(2)], (near_v, far_v))
        for d in range(1, plane):
            kernel_slice(d, False).start()

    near_all[l, s] = near_v[l]
    for d in range(1, plane):
        kernel_slice(d, True).start()
    far_all[l, s] = far_v[l]

    def arrived(i, _):
        group, block = i // n, lax.rem(i, n)

        @pl.when(jnp.logical_or(group != s, lax.rem(block, layers) != l))
        def _():
            probe_arrive(group, block).wait()

        return 0

    lax.fori_loop(0, groups * n, arrived, 0)

    def contract(everything, vectors):
        depth, columns = vectors.shape[0] * vectors.shape[1], vectors.shape[2]
        total = None
        for q in range(layers):
            part = lax.dot_general(
                everything[q].reshape(depth, everything.shape[3]),
                vectors.reshape(depth, columns),
                (((0,), (0,)), ((), ())),
                preferred_element_type=jnp.float32,
            )
            total = part if total is None else total + part
        return total

    for d in range(1, plane):
        kernel_arrive(d, False).wait()
    near_vectors = probe_v[:, 0:n - 2]
    near = contract(
        near_all,
        near_vectors.reshape(groups, (n - 2) * probe_v.shape[2], probe_v.shape[3]),
    )

    def sent(block, _):
        @pl.when(lax.rem(block, layers) == l)
        def _():
            for d in range(1, plane):
                relay_probe(block, d).wait_send()

            @pl.when(jnp.logical_and(has_up, block <= b))
            def _():
                line_probe(block, True).wait_send()

            @pl.when(jnp.logical_and(has_down, block >= b))
            def _():
                line_probe(block, False).wait_send()

        return 0

    lax.fori_loop(0, n, sent, 0)
    for block, going_up, has in ((n - 1, False, has_down), (0, True, has_up)):

        @pl.when(has)
        def _():
            for a, c in items[-flight:]:
                forward(a, c, block, going_up).wait_send()

    for d in range(1, plane):
        kernel_slice(d, False).wait_send()
    for d in range(1, plane):
        kernel_arrive(d, True).wait()
    far_vectors = probe_v[:, n - 2:n]
    far = contract(
        far_all,
        far_vectors.reshape(groups, 2 * probe_v.shape[2], probe_v.shape[3]),
    )
    out[...] = (near + far) * jnp.float32(scale)
    for d in range(1, plane):
        kernel_slice(d, True).wait_send()


def on_device(resident_act, resident_grad, source_act, source_grad, probes):
    n = lax.axis_size("blk")
    groups = lax.axis_size("src")
    layers = lax.axis_size("layer")
    _, rows, width = resident_act.shape
    per = source_act.shape[1]
    columns = probes.shape[1]
    source_total = per * n * groups
    total_layers = resident_act.shape[0] * layers
    share = rows // layers
    plane = groups * layers
    chunks = max(1, min(4, 16 // n))
    flight = min(3, 2 * chunks)
    body = functools.partial(
        kernel_body, n, groups, layers, chunks, flight, 1.0 / width,
        (total_layers * source_total) ** (-0.5),
    )
    dma = pltpu.SemaphoreType.DMA
    return pl.pallas_call(
        body,
        out_shape=jax.ShapeDtypeStruct((share, columns), jnp.float32),
        in_specs=[pl.BlockSpec(memory_space=pl.ANY)] * 5,
        out_specs=pl.BlockSpec(memory_space=pltpu.VMEM),
        scratch_shapes=[
            pltpu.VMEM((2, rows, width), jnp.bfloat16),
            pltpu.VMEM((2, n, per, width), jnp.bfloat16),
            pltpu.VMEM((groups, n, per, columns), jnp.bfloat16),
            pltpu.VMEM((layers, (n - 2) * per, share), jnp.bfloat16),
            pltpu.VMEM((layers, 2 * per, share), jnp.bfloat16),
            pltpu.VMEM((layers, groups, (n - 2) * per, share), jnp.bfloat16),
            pltpu.VMEM((layers, groups, 2 * per, share), jnp.bfloat16),
            dma((2, chunks)),
            dma((2,)),
            dma((2, chunks, n)),
            dma((2, chunks, n)),
            dma((2, chunks, n)),
            dma((groups, n)),
            dma((n,)),
            dma((n,)),
            dma((n, plane)),
            dma((plane,)),
            dma((plane,)),
            dma((plane,)),
            dma((plane,)),
        ],
        compiler_params=pltpu.CompilerParams(
            collective_id=0, has_side_effects=True, vmem_limit_bytes=56 * 1024 * 1024
        ),
        cost_estimate=pl.CostEstimate(
            flops=4 * n * per * rows * width,
            bytes_accessed=4 * rows * width,
            transcendentals=0,
        ),
        name="ntk_product",
    )(resident_act, resident_grad, source_act, source_grad, probes)


def solution(mesh):
    in_specs = (
        P("layer", "blk", None),
        P("layer", "blk", None),
        P("layer", ("blk", "src"), None),
        P("layer", ("blk", "src"), None),
        P(("blk", "src"), None),
    )
    out_specs = P(("blk", "layer"), None)
    return jax.shard_map(
        on_device, mesh=mesh, in_specs=in_specs, out_specs=out_specs, check_vma=False
    )
```

```python
import functools

import jax
import jax.numpy as jnp
from jax import lax
from jax.experimental import pallas as pl
from jax.experimental.pallas import tpu as pltpu
from jax.sharding import PartitionSpec as P

MESH = pl.DeviceIdType.MESH


def kernel_body(
    n, groups, layers, chunks, flight, inverse_width, scale,
    res_a, res_g, src_a, src_g, probes, out,
    res_v, src_v, probe_v, near_v, far_v, near_all, far_all,
    res_sem, own_sem, recv_sem, up_sem, down_sem,
    probe_sem, line_up, line_down, relay_sem,
    near_sem, near_send, far_sem, far_send,
):
    b = lax.axis_index("blk")
    s = lax.axis_index("src")
    l = lax.axis_index("layer")
    plane = groups * layers
    me = s * layers + l
    up = lax.rem(b + 1, n)
    down = lax.rem(b + n - 1, n)
    width = res_v.shape[2]
    step = width // chunks
    residents = (res_a, res_g)
    sources = (src_a, src_g)
    items = [(a, c) for a in range(2) for c in range(chunks)]
    has_up = b < n - 1
    has_down = b > 0

    def slot(position, block):
        return jnp.where(2 * position < n, block, n - 1 - block)

    def device_of(other):
        return (b, other // layers, lax.rem(other, layers))

    def peer(d):
        return device_of(lax.rem(me + d, plane))

    def cols(c):
        return pl.ds(c * step, step)

    def resident_copy(a, c):
        return pltpu.make_async_copy(
            residents[a].at[0, :, cols(c)], res_v.at[a, :, cols(c)], res_sem.at[a, c]
        )

    def own_copy(a):
        return pltpu.make_async_copy(
            sources[a].at[0], src_v.at[a, slot(b, b)], own_sem.at[a]
        )

    def move(source, a, c, block, going_up):
        to = up if going_up else down
        return pltpu.make_async_remote_copy(
            src_ref=source,
            dst_ref=src_v.at[a, slot(to, block), :, cols(c)],
            send_sem=(up_sem if going_up else down_sem).at[a, c, block],
            recv_sem=recv_sem.at[a, c, block],
            device_id=(to, s, l),
            device_id_type=MESH,
        )

    def own(a, c, going_up):
        return move(sources[a].at[0, :, cols(c)], a, c, b, going_up)

    def forward(a, c, block, going_up):
        return move(src_v.at[a, slot(b, block), :, cols(c)], a, c, block, going_up)

    def arrive(a, c, block):
        here = src_v.at[a, slot(b, block), :, cols(c)]
        return pltpu.make_async_copy(here, here, recv_sem.at[a, c, block])

    def line_probe(block, going_up, source=None):
        to = up if going_up else down
        return pltpu.make_async_remote_copy(
            src_ref=probe_v.at[s, slot(b, block)] if source is None else source,
            dst_ref=probe_v.at[s, slot(to, block)],
            send_sem=(line_up if going_up else line_down).at[block],
            recv_sem=probe_sem.at[s, block],
            device_id=(to, s, l),
            device_id_type=MESH,
        )

    def own_probe():
        return pltpu.make_async_copy(
            probes, probe_v.at[s, slot(b, b)], probe_sem.at[s, b]
        )

    def probe_arrive(group, block):
        here = probe_v.at[group, slot(b, block)]
        return pltpu.make_async_copy(here, here, probe_sem.at[group, block])

    def relay_probe(block, d):
        here = probe_v.at[s, slot(b, block)]
        return pltpu.make_async_remote_copy(
            src_ref=here,
            dst_ref=here,
            send_sem=relay_sem.at[block, d],
            recv_sem=probe_sem.at[s, block],
            device_id=peer(d),
            device_id_type=MESH,
        )

    def kernel_slice(d, far):
        device = peer(d)
        return pltpu.make_async_remote_copy(
            src_ref=(far_v if far else near_v).at[device[2]],
            dst_ref=(far_all if far else near_all).at[l, s],
            send_sem=(far_send if far else near_send).at[d],
            recv_sem=(far_sem if far else near_sem).at[me],
            device_id=device,
            device_id_type=MESH,
        )

    def kernel_arrive(d, far):
        other = lax.rem(me + d, plane)
        _, from_group, from_layer = device_of(other)
        here = (far_all if far else near_all).at[from_layer, from_group]
        return pltpu.make_async_copy(here, here, (far_sem if far else near_sem).at[other])

    def signal(device):
        pl.semaphore_signal(
            pltpu.get_barrier_semaphore(), inc=1, device_id=device, device_id_type=MESH
        )

    @pl.when(has_down)
    def _():
        signal((down, s, l))

    @pl.when(has_up)
    def _():
        signal((up, s, l))

    for d in range(1, plane):
        signal(peer(d))
    carries = lax.rem(b, layers) == l

    @pl.when(carries)
    def _():
        own_probe().start()

    for a in range(2):
        own_copy(a).start()
    for a, c in items:
        resident_copy(a, c).start()
    pl.semaphore_wait(
        pltpu.get_barrier_semaphore(),
        plane - 1 + has_up.astype(jnp.int32) + has_down.astype(jnp.int32),
    )

    @pl.when(jnp.logical_and(carries, has_down))
    def _():
        line_probe(b, False, probes).start()

    @pl.when(jnp.logical_and(carries, has_up))
    def _():
        line_probe(b, True, probes).start()

    for k, (a, c) in enumerate(items):
        for going_up, has in ((False, has_down), (True, has_up)):

            @pl.when(has)
            def _():
                if k >= flight:
                    forward(*items[k - flight], b, going_up).wait_send()
                own(a, c, going_up).start()

    def forwarding(turn, _):
        low = b - 1 - turn
        high = b + 1 + turn
        for block, inside, going_up, has in (
            (high, high < n, False, has_down),
            (low, low >= 0, True, has_up),
        ):
            probe_here = jnp.logical_and(inside, lax.rem(jnp.maximum(block, 0), layers) == l)

            @pl.when(probe_here)
            def _():
                probe_arrive(s, block).wait()

            @pl.when(jnp.logical_and(probe_here, has))
            def _():
                line_probe(block, going_up).start()

        for k, (a, c) in enumerate(items):
            for block, inside, going_up, has in (
                (high, high < n, False, has_down),
                (low, low >= 0, True, has_up),
            ):
                before = items[k - flight]
                earlier = block if k >= flight else (block + 1 if going_up else block - 1)

                @pl.when(inside)
                def _():
                    arrive(a, c, block).wait()

                @pl.when(jnp.logical_and(inside, has))
                def _():
                    forward(*before, earlier, going_up).wait_send()
                    forward(a, c, block, going_up).start()

        return 0

    at_end = jnp.logical_or(b == 0, b == n - 1)
    lax.fori_loop(0, n - 3, forwarding, 0)
    for a in range(2):
        own_copy(a).wait()

    def product(grams, buffers):
        kernel = (grams[0] * grams[1] * jnp.float32(inverse_width)).astype(jnp.bfloat16)
        share = kernel.shape[1] // layers
        row = 0
        for buffer in buffers:
            rows = buffer.shape[1]
            for q in range(layers):
                buffer[q] = kernel[row:row + rows, q * share:(q + 1) * share]
            row += rows

    def gram(a, first, last, ready):
        total = None
        for c in range(chunks):
            ready(a, c)
            block = src_v[a, first:last, :, c * step:(c + 1) * step]
            part = lax.dot_general(
                block.reshape(block.shape[0] * block.shape[1], step),
                res_v[a, :, c * step:(c + 1) * step],
                (((1,), (1,)), ((), ())),
                preferred_element_type=jnp.float32,
            )
            total = part if total is None else total + part
        return total

    def resident_ready(a, c):
        resident_copy(a, c).wait()

    def farthest_ready(a, c):
        for distance in (n - 2, n - 1):
            arrive(a, c, jnp.where(b == 0, distance, n - 1 - distance)).wait()

    @pl.when(at_end)
    def _():
        product([gram(a, 0, n - 2, resident_ready) for a in range(2)], (near_v,))
        for d in range(1, plane):
            kernel_slice(d, False).start()

    @pl.when(jnp.logical_not(at_end))
    def _():
        forwarding(n - 3, 0)

    def relay(block, _):
        @pl.when(lax.rem(block, layers) == l)
        def _():
            gap = jnp.abs(block - b)
            unseen = jnp.logical_and(at_end, gap >= n - 2)

            @pl.when(jnp.logical_or(block == b, unseen))
            def _():
                probe_arrive(s, block).wait()

            for d in range(1, plane):
                relay_probe(block, d).start()

        return 0

    lax.fori_loop(0, n, relay, 0)

    @pl.when(at_end)
    def _():
        product([gram(a, n - 2, n, farthest_ready) for a in range(2)], (far_v,))

    @pl.when(jnp.logical_not(at_end))
    def _():
        product([gram(a, 0, n, resident_ready) for a in range(2)], (near_v, far_v))
        for d in range(1, plane):
            kernel_slice(d, False).start()

    near_all[l, s] = near_v[l]
    for d in range(1, plane):
        kernel_slice(d, True).start()
    far_all[l, s] = far_v[l]

    def arrived(i, _):
        group, block = i // n, lax.rem(i, n)

        @pl.when(jnp.logical_or(group != s, lax.rem(block, layers) != l))
        def _():
            probe_arrive(group, block).wait()

        return 0

    lax.fori_loop(0, groups * n, arrived, 0)

    def contract(everything, vectors):
        depth, columns = vectors.shape[0] * vectors.shape[1], vectors.shape[2]
        total = None
        for q in range(layers):
            part = lax.dot_general(
                everything[q].reshape(depth, everything.shape[3]),
                vectors.reshape(depth, columns),
                (((0,), (0,)), ((), ())),
                preferred_element_type=jnp.float32,
            )
            total = part if total is None else total + part
        return total

    for d in range(1, plane):
        kernel_arrive(d, False).wait()
    near_vectors = probe_v[:, 0:n - 2]
    near = contract(
        near_all,
        near_vectors.reshape(groups, (n - 2) * probe_v.shape[2], probe_v.shape[3]),
    )

    def sent(block, _):
        @pl.when(lax.rem(block, layers) == l)
        def _():
            for d in range(1, plane):
                relay_probe(block, d).wait_send()

            @pl.when(jnp.logical_and(has_up, block <= b))
            def _():
                line_probe(block, True).wait_send()

            @pl.when(jnp.logical_and(has_down, block >= b))
            def _():
                line_probe(block, False).wait_send()

        return 0

    lax.fori_loop(0, n, sent, 0)
    for block, going_up, has in ((n - 1, False, has_down), (0, True, has_up)):

        @pl.when(has)
        def _():
            for a, c in items[-flight:]:
                forward(a, c, block, going_up).wait_send()

    for d in range(1, plane):
        kernel_slice(d, False).wait_send()
    for d in range(1, plane):
        kernel_arrive(d, True).wait()
    far_vectors = probe_v[:, n - 2:n]
    far = contract(
        far_all,
        far_vectors.reshape(groups, 2 * probe_v.shape[2], probe_v.shape[3]),
    )
    out[...] = (near + far) * jnp.float32(scale)
    for d in range(1, plane):
        kernel_slice(d, True).wait_send()


def on_device(resident_act, resident_grad, source_act, source_grad, probes):
    n = lax.axis_size("blk")
    groups = lax.axis_size("src")
    layers = lax.axis_size("layer")
    _, rows, width = resident_act.shape
    per = source_act.shape[1]
    columns = probes.shape[1]
    source_total = per * n * groups
    total_layers = resident_act.shape[0] * layers
    share = rows // layers
    plane = groups * layers
    chunks = max(1, min(4, 16 // n))
    flight = 2 * chunks
    body = functools.partial(
        kernel_body, n, groups, layers, chunks, flight, 1.0 / width,
        (total_layers * source_total) ** (-0.5),
    )
    dma = pltpu.SemaphoreType.DMA
    return pl.pallas_call(
        body,
        out_shape=jax.ShapeDtypeStruct((share, columns), jnp.float32),
        in_specs=[pl.BlockSpec(memory_space=pl.ANY)] * 5,
        out_specs=pl.BlockSpec(memory_space=pltpu.VMEM),
        scratch_shapes=[
            pltpu.VMEM((2, rows, width), jnp.bfloat16),
            pltpu.VMEM((2, n, per, width), jnp.bfloat16),
            pltpu.VMEM((groups, n, per, columns), jnp.bfloat16),
            pltpu.VMEM((layers, (n - 2) * per, share), jnp.bfloat16),
            pltpu.VMEM((layers, 2 * per, share), jnp.bfloat16),
            pltpu.VMEM((layers, groups, (n - 2) * per, share), jnp.bfloat16),
            pltpu.VMEM((layers, groups, 2 * per, share), jnp.bfloat16),
            dma((2, chunks)),
            dma((2,)),
            dma((2, chunks, n)),
            dma((2, chunks, n)),
            dma((2, chunks, n)),
            dma((groups, n)),
            dma((n,)),
            dma((n,)),
            dma((n, plane)),
            dma((plane,)),
            dma((plane,)),
            dma((plane,)),
            dma((plane,)),
        ],
        compiler_params=pltpu.CompilerParams(
            collective_id=0, has_side_effects=True, vmem_limit_bytes=56 * 1024 * 1024
        ),
        cost_estimate=pl.CostEstimate(
            flops=4 * n * per * rows * width,
            bytes_accessed=4 * rows * width,
            transcendentals=0,
        ),
        name="ntk_product",
    )(resident_act, resident_grad, source_act, source_grad, probes)


def solution(mesh):
    in_specs = (
        P("layer", "blk", None),
        P("layer", "blk", None),
        P("layer", ("blk", "src"), None),
        P("layer", ("blk", "src"), None),
        P(("blk", "src"), None),
    )
    out_specs = P(("blk", "layer"), None)
    return jax.shard_map(
        on_device, mesh=mesh, in_specs=in_specs, out_specs=out_specs, check_vma=False
    )
```

```python
import functools

import jax
import jax.numpy as jnp
from jax import lax
from jax.experimental import pallas as pl
from jax.experimental.pallas import tpu as pltpu
from jax.sharding import PartitionSpec as P

MESH = pl.DeviceIdType.MESH


def kernel_body(
    n, groups, layers, chunks, flight, inverse_width, scale,
    res_a, res_g, src_a, src_g, probes, out,
    res_v, src_v, probe_v, near_v, far_v, near_all, far_all,
    res_sem, own_sem, recv_sem, up_sem, down_sem,
    probe_sem, line_up, line_down, relay_sem,
    near_sem, near_send, far_sem, far_send,
):
    b = lax.axis_index("blk")
    s = lax.axis_index("src")
    l = lax.axis_index("layer")
    plane = groups * layers
    me = s * layers + l
    up = lax.rem(b + 1, n)
    down = lax.rem(b + n - 1, n)
    width = res_v.shape[2]
    step = width // chunks
    residents = (res_a, res_g)
    sources = (src_a, src_g)
    items = [(a, c) for a in range(2) for c in range(chunks)]
    has_up = b < n - 1
    has_down = b > 0

    def slot(position, block):
        return jnp.where(2 * position < n, block, n - 1 - block)

    def device_of(other):
        return (b, other // layers, lax.rem(other, layers))

    def peer(d):
        return device_of(lax.rem(me + d, plane))

    def cols(c):
        return pl.ds(c * step, step)

    def resident_copy(a, c):
        return pltpu.make_async_copy(
            residents[a].at[0, :, cols(c)], res_v.at[a, :, cols(c)], res_sem.at[a, c]
        )

    def own_copy(a):
        return pltpu.make_async_copy(
            sources[a].at[0], src_v.at[a, slot(b, b)], own_sem.at[a]
        )

    def move(source, a, c, block, going_up):
        to = up if going_up else down
        return pltpu.make_async_remote_copy(
            src_ref=source,
            dst_ref=src_v.at[a, slot(to, block), :, cols(c)],
            send_sem=(up_sem if going_up else down_sem).at[a, c, block],
            recv_sem=recv_sem.at[a, c, block],
            device_id=(to, s, l),
            device_id_type=MESH,
        )

    def own(a, c, going_up):
        return move(sources[a].at[0, :, cols(c)], a, c, b, going_up)

    def forward(a, c, block, going_up):
        return move(src_v.at[a, slot(b, block), :, cols(c)], a, c, block, going_up)

    def arrive(a, c, block):
        here = src_v.at[a, slot(b, block), :, cols(c)]
        return pltpu.make_async_copy(here, here, recv_sem.at[a, c, block])

    def line_probe(block, going_up, source=None):
        to = up if going_up else down
        return pltpu.make_async_remote_copy(
            src_ref=probe_v.at[s, slot(b, block)] if source is None else source,
            dst_ref=probe_v.at[s, slot(to, block)],
            send_sem=(line_up if going_up else line_down).at[block],
            recv_sem=probe_sem.at[s, block],
            device_id=(to, s, l),
            device_id_type=MESH,
        )

    def own_probe():
        return pltpu.make_async_copy(
            probes, probe_v.at[s, slot(b, b)], probe_sem.at[s, b]
        )

    def probe_arrive(group, block):
        here = probe_v.at[group, slot(b, block)]
        return pltpu.make_async_copy(here, here, probe_sem.at[group, block])

    def relay_probe(block, d):
        here = probe_v.at[s, slot(b, block)]
        return pltpu.make_async_remote_copy(
            src_ref=here,
            dst_ref=here,
            send_sem=relay_sem.at[block, d],
            recv_sem=probe_sem.at[s, block],
            device_id=peer(d),
            device_id_type=MESH,
        )

    def kernel_slice(d, far):
        device = peer(d)
        return pltpu.make_async_remote_copy(
            src_ref=(far_v if far else near_v).at[device[2]],
            dst_ref=(far_all if far else near_all).at[l, s],
            send_sem=(far_send if far else near_send).at[d],
            recv_sem=(far_sem if far else near_sem).at[me],
            device_id=device,
            device_id_type=MESH,
        )

    def kernel_arrive(d, far):
        other = lax.rem(me + d, plane)
        _, from_group, from_layer = device_of(other)
        here = (far_all if far else near_all).at[from_layer, from_group]
        return pltpu.make_async_copy(here, here, (far_sem if far else near_sem).at[other])

    def signal(device):
        pl.semaphore_signal(
            pltpu.get_barrier_semaphore(), inc=1, device_id=device, device_id_type=MESH
        )

    @pl.when(has_down)
    def _():
        signal((down, s, l))

    @pl.when(has_up)
    def _():
        signal((up, s, l))

    for d in range(1, plane):
        signal(peer(d))
    carries = lax.rem(b, layers) == l

    @pl.when(carries)
    def _():
        own_probe().start()

    for a in range(2):
        own_copy(a).start()
    for a, c in items:
        resident_copy(a, c).start()
    pl.semaphore_wait(
        pltpu.get_barrier_semaphore(),
        plane - 1 + has_up.astype(jnp.int32) + has_down.astype(jnp.int32),
    )

    @pl.when(jnp.logical_and(carries, has_down))
    def _():
        line_probe(b, False, probes).start()

    @pl.when(jnp.logical_and(carries, has_up))
    def _():
        line_probe(b, True, probes).start()

    for k, (a, c) in enumerate(items):
        for going_up, has in ((False, has_down), (True, has_up)):

            @pl.when(has)
            def _():
                if k >= flight:
                    forward(*items[k - flight], b, going_up).wait_send()
                own(a, c, going_up).start()

    def forwarding(turn, _):
        low = b - 1 - turn
        high = b + 1 + turn
        for block, inside, going_up, has in (
            (high, high < n, False, has_down),
            (low, low >= 0, True, has_up),
        ):
            probe_here = jnp.logical_and(inside, lax.rem(jnp.maximum(block, 0), layers) == l)

            @pl.when(probe_here)
            def _():
                probe_arrive(s, block).wait()

            @pl.when(jnp.logical_and(probe_here, has))
            def _():
                line_probe(block, going_up).start()

        for k, (a, c) in enumerate(items):
            for block, inside, going_up, has in (
                (high, high < n, False, has_down),
                (low, low >= 0, True, has_up),
            ):
                before = items[k - flight]
                earlier = block if k >= flight else (block + 1 if going_up else block - 1)

                @pl.when(inside)
                def _():
                    arrive(a, c, block).wait()

                @pl.when(jnp.logical_and(inside, has))
                def _():
                    forward(*before, earlier, going_up).wait_send()
                    forward(a, c, block, going_up).start()

        return 0

    at_end = jnp.logical_or(b == 0, b == n - 1)
    lax.fori_loop(0, n - 3, forwarding, 0)
    for a in range(2):
        own_copy(a).wait()

    def product(grams, buffers):
        kernel = (grams[0] * grams[1] * jnp.float32(inverse_width)).astype(jnp.bfloat16)
        share = kernel.shape[1] // layers
        row = 0
        for buffer in buffers:
            rows = buffer.shape[1]
            for q in range(layers):
                buffer[q] = kernel[row:row + rows, q * share:(q + 1) * share]
            row += rows

    def gram(a, first, last, ready):
        total = None
        for c in range(chunks):
            ready(a, c)
            block = src_v[a, first:last, :, c * step:(c + 1) * step]
            part = lax.dot_general(
                block.reshape(block.shape[0] * block.shape[1], step),
                res_v[a, :, c * step:(c + 1) * step],
                (((1,), (1,)), ((), ())),
                preferred_element_type=jnp.float32,
            )
            total = part if total is None else total + part
        return total

    def resident_ready(a, c):
        resident_copy(a, c).wait()

    def farthest_ready(a, c):
        for distance in (n - 2, n - 1):
            arrive(a, c, jnp.where(b == 0, distance, n - 1 - distance)).wait()

    @pl.when(at_end)
    def _():
        product([gram(a, 0, n - 2, resident_ready) for a in range(2)], (near_v,))
        for d in range(1, plane):
            kernel_slice(d, False).start()

    @pl.when(jnp.logical_not(at_end))
    def _():
        forwarding(n - 3, 0)

    def relay(block, _):
        @pl.when(lax.rem(block, layers) == l)
        def _():
            gap = jnp.abs(block - b)
            unseen = jnp.logical_and(at_end, gap >= n - 2)

            @pl.when(jnp.logical_or(block == b, unseen))
            def _():
                probe_arrive(s, block).wait()

            for d in range(1, plane):
                relay_probe(block, d).start()

        return 0

    lax.fori_loop(0, n, relay, 0)

    @pl.when(at_end)
    def _():
        product([gram(a, n - 2, n, farthest_ready) for a in range(2)], (far_v,))

    @pl.when(jnp.logical_not(at_end))
    def _():
        product([gram(a, 0, n, resident_ready) for a in range(2)], (near_v, far_v))
        for d in range(1, plane):
            kernel_slice(d, False).start()

    near_all[l, s] = near_v[l]
    for d in range(1, plane):
        kernel_slice(d, True).start()
    far_all[l, s] = far_v[l]

    def arrived(i, _):
        group, block = i // n, lax.rem(i, n)

        @pl.when(jnp.logical_or(group != s, lax.rem(block, layers) != l))
        def _():
            probe_arrive(group, block).wait()

        return 0

    lax.fori_loop(0, groups * n, arrived, 0)

    def contract(everything, vectors):
        depth, columns = vectors.shape[0] * vectors.shape[1], vectors.shape[2]
        total = None
        for q in range(layers):
            part = lax.dot_general(
                everything[q].reshape(depth, everything.shape[3]),
                vectors.reshape(depth, columns),
                (((0,), (0,)), ((), ())),
                preferred_element_type=jnp.float32,
            )
            total = part if total is None else total + part
        return total

    for d in range(1, plane):
        kernel_arrive(d, False).wait()
    near_vectors = probe_v[:, 0:n - 2]
    near = contract(
        near_all,
        near_vectors.reshape(groups, (n - 2) * probe_v.shape[2], probe_v.shape[3]),
    )

    def sent(block, _):
        @pl.when(lax.rem(block, layers) == l)
        def _():
            for d in range(1, plane):
                relay_probe(block, d).wait_send()

            @pl.when(jnp.logical_and(has_up, block <= b))
            def _():
                line_probe(block, True).wait_send()

            @pl.when(jnp.logical_and(has_down, block >= b))
            def _():
                line_probe(block, False).wait_send()

        return 0

    lax.fori_loop(0, n, sent, 0)
    for block, going_up, has in ((n - 1, False, has_down), (0, True, has_up)):

        @pl.when(has)
        def _():
            for a, c in items[-flight:]:
                forward(a, c, block, going_up).wait_send()

    for d in range(1, plane):
        kernel_slice(d, False).wait_send()
    for d in range(1, plane):
        kernel_arrive(d, True).wait()
    far_vectors = probe_v[:, n - 2:n]
    far = contract(
        far_all,
        far_vectors.reshape(groups, 2 * probe_v.shape[2], probe_v.shape[3]),
    )
    out[...] = near + far
    for d in range(1, plane):
        kernel_slice(d, True).wait_send()


def on_device(resident_act, resident_grad, source_act, source_grad, probes):
    n = lax.axis_size("blk")
    groups = lax.axis_size("src")
    layers = lax.axis_size("layer")
    _, rows, width = resident_act.shape
    per = source_act.shape[1]
    columns = probes.shape[1]
    source_total = per * n * groups
    total_layers = resident_act.shape[0] * layers
    share = rows // layers
    plane = groups * layers
    chunks = max(1, min(4, 16 // n))
    flight = min(5, 2 * chunks)
    body = functools.partial(
        kernel_body, n, groups, layers, chunks, flight, 1.0 / width,
        (total_layers * source_total) ** (-0.5),
    )
    dma = pltpu.SemaphoreType.DMA
    total = pl.pallas_call(
        body,
        out_shape=pltpu.VMEM((share, columns), jnp.float32),
        in_specs=[pl.BlockSpec(memory_space=pl.ANY)] * 5,
        out_specs=pl.BlockSpec(memory_space=pltpu.VMEM),
        scratch_shapes=[
            pltpu.VMEM((2, rows, width), jnp.bfloat16),
            pltpu.VMEM((2, n, per, width), jnp.bfloat16),
            pltpu.VMEM((groups, n, per, columns), jnp.bfloat16),
            pltpu.VMEM((layers, (n - 2) * per, share), jnp.bfloat16),
            pltpu.VMEM((layers, 2 * per, share), jnp.bfloat16),
            pltpu.VMEM((layers, groups, (n - 2) * per, share), jnp.bfloat16),
            pltpu.VMEM((layers, groups, 2 * per, share), jnp.bfloat16),
            dma((2, chunks)),
            dma((2,)),
            dma((2, chunks, n)),
            dma((2, chunks, n)),
            dma((2, chunks, n)),
            dma((groups, n)),
            dma((n,)),
            dma((n,)),
            dma((n, plane)),
            dma((plane,)),
            dma((plane,)),
            dma((plane,)),
            dma((plane,)),
        ],
        compiler_params=pltpu.CompilerParams(
            collective_id=0, has_side_effects=True, vmem_limit_bytes=56 * 1024 * 1024
        ),
        cost_estimate=pl.CostEstimate(
            flops=4 * n * per * rows * width,
            bytes_accessed=4 * rows * width,
            transcendentals=0,
        ),
        name="ntk_product",
    )(resident_act, resident_grad, source_act, source_grad, probes)
    return total * jnp.float32((total_layers * source_total) ** (-0.5))


def solution(mesh):
    in_specs = (
        P("layer", "blk", None),
        P("layer", "blk", None),
        P("layer", ("blk", "src"), None),
        P("layer", ("blk", "src"), None),
        P(("blk", "src"), None),
    )
    out_specs = P(("blk", "layer"), None)
    return jax.shard_map(
        on_device, mesh=mesh, in_specs=in_specs, out_specs=out_specs, check_vma=False
    )
```

```python
import functools

import jax
import jax.numpy as jnp
from jax import lax
from jax.experimental import pallas as pl
from jax.experimental.pallas import tpu as pltpu
from jax.sharding import PartitionSpec as P

MESH = pl.DeviceIdType.MESH


def kernel_body(
    n, groups, layers, chunks, flight, inverse_width, scale,
    res_a, res_g, src_a, src_g, probes, out,
    res_v, src_v, probe_v, near_v, far_v, near_all, far_all,
    res_sem, own_sem, recv_sem, up_sem, down_sem,
    probe_sem, line_up, line_down, relay_sem,
    near_sem, near_send, far_sem, far_send,
):
    b = lax.axis_index("blk")
    s = lax.axis_index("src")
    l = lax.axis_index("layer")
    plane = groups * layers
    me = s * layers + l
    up = lax.rem(b + 1, n)
    down = lax.rem(b + n - 1, n)
    width = res_v.shape[2]
    step = width // chunks
    residents = (res_a, res_g)
    sources = (src_a, src_g)
    items = [(a, c) for a in range(2) for c in range(chunks)]
    has_up = b < n - 1
    has_down = b > 0

    def slot(position, block):
        return jnp.where(2 * position < n, block, n - 1 - block)

    def device_of(other):
        return (b, other // layers, lax.rem(other, layers))

    def peer(d):
        return device_of(lax.rem(me + d, plane))

    def cols(c):
        return pl.ds(c * step, step)

    def resident_copy(a, c):
        return pltpu.make_async_copy(
            residents[a].at[0, :, cols(c)], res_v.at[a, :, cols(c)], res_sem.at[a, c]
        )

    def own_copy(a):
        return pltpu.make_async_copy(
            sources[a].at[0], src_v.at[a, slot(b, b)], own_sem.at[a]
        )

    def move(source, a, c, block, going_up):
        to = up if going_up else down
        return pltpu.make_async_remote_copy(
            src_ref=source,
            dst_ref=src_v.at[a, slot(to, block), :, cols(c)],
            send_sem=(up_sem if going_up else down_sem).at[a, c, block],
            recv_sem=recv_sem.at[a, c, block],
            device_id=(to, s, l),
            device_id_type=MESH,
        )

    def own(a, c, going_up):
        return move(sources[a].at[0, :, cols(c)], a, c, b, going_up)

    def forward(a, c, block, going_up):
        return move(src_v.at[a, slot(b, block), :, cols(c)], a, c, block, going_up)

    def arrive(a, c, block):
        here = src_v.at[a, slot(b, block), :, cols(c)]
        return pltpu.make_async_copy(here, here, recv_sem.at[a, c, block])

    def line_probe(block, going_up, source=None):
        to = up if going_up else down
        return pltpu.make_async_remote_copy(
            src_ref=probe_v.at[s, slot(b, block)] if source is None else source,
            dst_ref=probe_v.at[s, slot(to, block)],
            send_sem=(line_up if going_up else line_down).at[block],
            recv_sem=probe_sem.at[s, block],
            device_id=(to, s, l),
            device_id_type=MESH,
        )

    def own_probe():
        return pltpu.make_async_copy(
            probes, probe_v.at[s, slot(b, b)], probe_sem.at[s, b]
        )

    def probe_arrive(group, block):
        here = probe_v.at[group, slot(b, block)]
        return pltpu.make_async_copy(here, here, probe_sem.at[group, block])

    def relay_probe(block, d):
        here = probe_v.at[s, slot(b, block)]
        return pltpu.make_async_remote_copy(
            src_ref=here,
            dst_ref=here,
            send_sem=relay_sem.at[block, d],
            recv_sem=probe_sem.at[s, block],
            device_id=peer(d),
            device_id_type=MESH,
        )

    def kernel_slice(d, far):
        device = peer(d)
        return pltpu.make_async_remote_copy(
            src_ref=(far_v if far else near_v).at[device[2]],
            dst_ref=(far_all if far else near_all).at[l, s],
            send_sem=(far_send if far else near_send).at[d],
            recv_sem=(far_sem if far else near_sem).at[me],
            device_id=device,
            device_id_type=MESH,
        )

    def kernel_arrive(d, far):
        other = lax.rem(me + d, plane)
        _, from_group, from_layer = device_of(other)
        here = (far_all if far else near_all).at[from_layer, from_group]
        return pltpu.make_async_copy(here, here, (far_sem if far else near_sem).at[other])

    def signal(device):
        pl.semaphore_signal(
            pltpu.get_barrier_semaphore(), inc=1, device_id=device, device_id_type=MESH
        )

    @pl.when(has_down)
    def _():
        signal((down, s, l))

    @pl.when(has_up)
    def _():
        signal((up, s, l))

    for d in range(1, plane):
        signal(peer(d))
    carries = lax.rem(b, layers) == l

    @pl.when(carries)
    def _():
        own_probe().start()

    for a in range(2):
        own_copy(a).start()
    for a, c in items:
        resident_copy(a, c).start()
    pl.semaphore_wait(
        pltpu.get_barrier_semaphore(),
        plane - 1 + has_up.astype(jnp.int32) + has_down.astype(jnp.int32),
    )

    @pl.when(jnp.logical_and(carries, has_down))
    def _():
        line_probe(b, False, probes).start()

    @pl.when(jnp.logical_and(carries, has_up))
    def _():
        line_probe(b, True, probes).start()

    for k, (a, c) in enumerate(items):
        for going_up, has in ((False, has_down), (True, has_up)):

            @pl.when(has)
            def _():
                if k >= flight:
                    forward(*items[k - flight], b, going_up).wait_send()
                own(a, c, going_up).start()

    def forwarding(turn, _):
        low = b - 1 - turn
        high = b + 1 + turn
        for block, inside, going_up, has in (
            (high, high < n, False, has_down),
            (low, low >= 0, True, has_up),
        ):
            probe_here = jnp.logical_and(inside, lax.rem(jnp.maximum(block, 0), layers) == l)

            @pl.when(probe_here)
            def _():
                probe_arrive(s, block).wait()

            @pl.when(jnp.logical_and(probe_here, has))
            def _():
                line_probe(block, going_up).start()

        for k, (a, c) in enumerate(items):
            for block, inside, going_up, has in (
                (high, high < n, False, has_down),
                (low, low >= 0, True, has_up),
            ):
                before = items[k - flight]
                earlier = block if k >= flight else (block + 1 if going_up else block - 1)

                @pl.when(inside)
                def _():
                    arrive(a, c, block).wait()

                @pl.when(jnp.logical_and(inside, has))
                def _():
                    forward(*before, earlier, going_up).wait_send()
                    forward(a, c, block, going_up).start()

        return 0

    at_end = jnp.logical_or(b == 0, b == n - 1)
    lax.fori_loop(0, n - 3, forwarding, 0)
    for a in range(2):
        own_copy(a).wait()

    def product(grams, buffers):
        kernel = (grams[0] * grams[1] * jnp.float32(inverse_width)).astype(jnp.bfloat16)
        share = kernel.shape[1] // layers
        row = 0
        for buffer in buffers:
            rows = buffer.shape[1]
            for q in range(layers):
                buffer[q] = kernel[row:row + rows, q * share:(q + 1) * share]
            row += rows

    def gram(a, first, last, ready):
        total = None
        for c in range(chunks):
            ready(a, c)
            block = src_v[a, first:last, :, c * step:(c + 1) * step]
            part = lax.dot_general(
                block.reshape(block.shape[0] * block.shape[1], step),
                res_v[a, :, c * step:(c + 1) * step],
                (((1,), (1,)), ((), ())),
                preferred_element_type=jnp.float32,
            )
            total = part if total is None else total + part
        return total

    def resident_ready(a, c):
        resident_copy(a, c).wait()

    def farthest_ready(a, c):
        for distance in (n - 2, n - 1):
            arrive(a, c, jnp.where(b == 0, distance, n - 1 - distance)).wait()

    @pl.when(at_end)
    def _():
        product([gram(a, 0, n - 2, resident_ready) for a in range(2)], (near_v,))
        for d in range(1, plane):
            kernel_slice(d, False).start()

    @pl.when(jnp.logical_not(at_end))
    def _():
        forwarding(n - 3, 0)

    def relay(block, _):
        @pl.when(lax.rem(block, layers) == l)
        def _():
            gap = jnp.abs(block - b)
            unseen = jnp.logical_and(at_end, gap >= n - 2)

            @pl.when(jnp.logical_or(block == b, unseen))
            def _():
                probe_arrive(s, block).wait()

            for d in range(1, plane):
                relay_probe(block, d).start()

        return 0

    lax.fori_loop(0, n, relay, 0)

    @pl.when(at_end)
    def _():
        product([gram(a, n - 2, n, farthest_ready) for a in range(2)], (far_v,))

    @pl.when(jnp.logical_not(at_end))
    def _():
        product([gram(a, 0, n, resident_ready) for a in range(2)], (near_v, far_v))
        for d in range(1, plane):
            kernel_slice(d, False).start()

    near_all[l, s] = near_v[l]
    for d in range(1, plane):
        kernel_slice(d, True).start()
    far_all[l, s] = far_v[l]

    def arrived(i, _):
        group, block = i // n, lax.rem(i, n)

        @pl.when(jnp.logical_or(group != s, lax.rem(block, layers) != l))
        def _():
            probe_arrive(group, block).wait()

        return 0

    lax.fori_loop(0, groups * n, arrived, 0)

    def contract(everything, vectors):
        depth, columns = vectors.shape[0] * vectors.shape[1], vectors.shape[2]
        total = None
        for q in range(layers):
            part = lax.dot_general(
                everything[q].reshape(depth, everything.shape[3]),
                vectors.reshape(depth, columns),
                (((0,), (0,)), ((), ())),
                preferred_element_type=jnp.float32,
            )
            total = part if total is None else total + part
        return total

    for d in range(1, plane):
        kernel_arrive(d, False).wait()
    near_vectors = probe_v[:, 0:n - 2]
    near = contract(
        near_all,
        near_vectors.reshape(groups, (n - 2) * probe_v.shape[2], probe_v.shape[3]),
    )

    def sent(block, _):
        @pl.when(lax.rem(block, layers) == l)
        def _():
            for d in range(1, plane):
                relay_probe(block, d).wait_send()

            @pl.when(jnp.logical_and(has_up, block <= b))
            def _():
                line_probe(block, True).wait_send()

            @pl.when(jnp.logical_and(has_down, block >= b))
            def _():
                line_probe(block, False).wait_send()

        return 0

    lax.fori_loop(0, n, sent, 0)
    for block, going_up, has in ((n - 1, False, has_down), (0, True, has_up)):

        @pl.when(has)
        def _():
            for a, c in items[-flight:]:
                forward(a, c, block, going_up).wait_send()

    for d in range(1, plane):
        kernel_slice(d, False).wait_send()
    for d in range(1, plane):
        kernel_arrive(d, True).wait()
    far_vectors = probe_v[:, n - 2:n]
    far = contract(
        far_all,
        far_vectors.reshape(groups, 2 * probe_v.shape[2], probe_v.shape[3]),
    )
    out[...] = near + far
    for d in range(1, plane):
        kernel_slice(d, True).wait_send()


def on_device(resident_act, resident_grad, source_act, source_grad, probes):
    n = lax.axis_size("blk")
    groups = lax.axis_size("src")
    layers = lax.axis_size("layer")
    _, rows, width = resident_act.shape
    per = source_act.shape[1]
    columns = probes.shape[1]
    source_total = per * n * groups
    total_layers = resident_act.shape[0] * layers
    share = rows // layers
    plane = groups * layers
    chunks = max(1, min(2, 16 // n))
    flight = min(3, 2 * chunks)
    body = functools.partial(
        kernel_body, n, groups, layers, chunks, flight, 1.0 / width,
        (total_layers * source_total) ** (-0.5),
    )
    dma = pltpu.SemaphoreType.DMA
    total = pl.pallas_call(
        body,
        out_shape=pltpu.VMEM((share, columns), jnp.float32),
        in_specs=[pl.BlockSpec(memory_space=pl.ANY)] * 5,
        out_specs=pl.BlockSpec(memory_space=pltpu.VMEM),
        scratch_shapes=[
            pltpu.VMEM((2, rows, width), jnp.bfloat16),
            pltpu.VMEM((2, n, per, width), jnp.bfloat16),
            pltpu.VMEM((groups, n, per, columns), jnp.bfloat16),
            pltpu.VMEM((layers, (n - 2) * per, share), jnp.bfloat16),
            pltpu.VMEM((layers, 2 * per, share), jnp.bfloat16),
            pltpu.VMEM((layers, groups, (n - 2) * per, share), jnp.bfloat16),
            pltpu.VMEM((layers, groups, 2 * per, share), jnp.bfloat16),
            dma((2, chunks)),
            dma((2,)),
            dma((2, chunks, n)),
            dma((2, chunks, n)),
            dma((2, chunks, n)),
            dma((groups, n)),
            dma((n,)),
            dma((n,)),
            dma((n, plane)),
            dma((plane,)),
            dma((plane,)),
            dma((plane,)),
            dma((plane,)),
        ],
        compiler_params=pltpu.CompilerParams(
            collective_id=0, has_side_effects=True, vmem_limit_bytes=56 * 1024 * 1024
        ),
        cost_estimate=pl.CostEstimate(
            flops=4 * n * per * rows * width,
            bytes_accessed=4 * rows * width,
            transcendentals=0,
        ),
        name="ntk_product",
    )(resident_act, resident_grad, source_act, source_grad, probes)
    return total * jnp.float32((total_layers * source_total) ** (-0.5))


def solution(mesh):
    in_specs = (
        P("layer", "blk", None),
        P("layer", "blk", None),
        P("layer", ("blk", "src"), None),
        P("layer", ("blk", "src"), None),
        P(("blk", "src"), None),
    )
    out_specs = P(("blk", "layer"), None)
    return jax.shard_map(
        on_device, mesh=mesh, in_specs=in_specs, out_specs=out_specs, check_vma=False
    )
```
